32 devices in a mesh: row: 4 (over y, x), col: 8 (over z, core).
Axes of the slice: x: 2, y: 2, z: 4, core: 2. Of those that a mesh axis runs over, the one named last changes fastest.
Arguments:
- embeddings: bfloat16 [16384, 768], P(('row', 'col'))
- counts: int32 [32], replicated, may hold values from 256 to 512
- pairs: int32 [32, 6], replicated, may hold values from 0 to 31, as said below
Outputs:
- density: float32 [16384], P(('row', 'col'))
- neighbour: bfloat16 [16384, 768], P(('row', 'col'))
The draws below stay inside these ranges and needn't reach their ends.
Inputs may be any that keep to these rules, and one draw needn't show every extreme that they name: Row b of pairs lists 6 different blocks; the first is b itself, each other is (b + o) mod 32 for an offset o with 1 <= |o| <= 4; some row lists the offset 4 and some row the offset minus 4.
All inputs are finite; a program needn't handle non-finite values.
Results may differ from the reference program's by a relative error of at most 0.0023.
Values may be sent and summed in bfloat16 or wider, within the bound.
A program may use at most 64 MiB of HBM per device.

```python
import jax
import jax.numpy as jnp
from jax import lax

D = 768
ROWS_DEV = 512
KP = 6
REACH = 4
NB = 32
NDOC = 16384


def draw_embeddings(key, part):
    key_center, key_member, key_noise = jax.random.split(jax.random.fold_in(key, 11), 3)
    centers = jax.random.normal(key_center, (16, D), jnp.float32)
    member = jax.random.randint(key_member, (NDOC,), 0, 16)
    noise = jax.random.normal(key_noise, (NDOC, D), jnp.float32)
    values = 0.8 * centers[member] + noise
    return values.astype(jnp.bfloat16)


def draw_counts(key, part):
    key_count, key_place = jax.random.split(jax.random.fold_in(key, 23))
    values = jax.random.randint(key_count, (NB,), ROWS_DEV // 2, ROWS_DEV + 1)
    places = jax.random.permutation(key_place, NB)
    values = values.at[places[0]].set(ROWS_DEV).at[places[1]].set(ROWS_DEV // 2)
    return values.astype(jnp.int32)


def draw_pairs(key, part):
    row_keys = jax.random.split(jax.random.fold_in(key, 37), NB)
    candidates = jnp.concatenate([jnp.arange(1, REACH + 1, dtype=jnp.int32), -jnp.arange(1, REACH + 1, dtype=jnp.int32)])
    picks = jax.vmap(lambda single: candidates[jax.random.permutation(single, 2 * REACH)[:KP - 1]])(row_keys)
    first_row = picks[0]
    first_row = jnp.where(jnp.any(first_row == REACH), first_row, first_row.at[0].set(REACH))
    second_row = picks[1]
    second_row = jnp.where(jnp.any(second_row == -REACH), second_row, second_row.at[0].set(-REACH))
    picks = picks.at[0].set(first_row).at[1].set(second_row)
    own = jnp.arange(NB, dtype=jnp.int32)[:, None]
    neighbour_embeddings = (own + picks + NB) % NB
    return jnp.concatenate([own, neighbour_embeddings], axis=1).astype(jnp.int32)


def setup_inputs(seed: int = 0) -> dict:
    arg_keys = jax.random.split(jax.random.key(seed), 4)
    return {
        "embeddings": draw_embeddings(jax.random.fold_in(arg_keys[3], 71), 0),
        "counts": draw_counts(jax.random.fold_in(arg_keys[3], 71), 0),
        "pairs": draw_pairs(jax.random.fold_in(arg_keys[3], 71), 0),
    }


smoothing_scale = 4.0
epsilon = 1e-06

def reference(embeddings, counts, pairs):
    flat = embeddings.astype(jnp.float32)
    inverse = lax.rsqrt(lax.optimization_barrier(jnp.sum(flat * flat, axis=1)) + epsilon)
    slot_index = jnp.arange(ROWS_DEV, dtype=jnp.int32)
    valid_mask = slot_index[None, :] < counts[:, None]
    tile_groups = embeddings.reshape(NB, ROWS_DEV, D)
    undo_tile_lookup = inverse.reshape(NB, ROWS_DEV)

    def one_block(index):
        row_block = tile_groups[index]
        chosen = pairs[index]
        col_blocks = tile_groups[chosen].reshape(KP * ROWS_DEV, D)
        col_inverse = undo_tile_lookup[chosen].reshape(KP * ROWS_DEV)
        target_entry_present = valid_mask[chosen].reshape(KP * ROWS_DEV)
        products = jnp.dot(row_block, col_blocks.T, preferred_element_type=jnp.float32)
        angular_agreement = products * undo_tile_lookup[index][:, None] * col_inverse[None, :]
        coupling_factor = jnp.where(target_entry_present[None, :], jnp.exp(smoothing_scale * (angular_agreement - 1.0)), 0.0)
        total = lax.optimization_barrier(jnp.sum(coupling_factor, axis=1))
        summed = jnp.dot(coupling_factor.astype(jnp.bfloat16), col_blocks, preferred_element_type=jnp.float32)
        row_valid = valid_mask[index]
        density = jnp.where(row_valid, total, 0.0)
        neighbour = jnp.where(row_valid[:, None], summed / total[:, None], 0.0).astype(jnp.bfloat16)
        return (density, neighbour)
    density, neighbour = lax.map(one_block, jnp.arange(NB, dtype=jnp.int32))
    return (density.reshape(NDOC), neighbour.reshape(NDOC, D))
```

```python
import functools
import math

import jax
import jax.numpy as jnp
from jax import lax
from jax.experimental import pallas as pl
from jax.experimental.pallas import tpu as pltpu
from jax.sharding import PartitionSpec as P

MESH = pl.DeviceIdType.MESH

smoothing_scale = 4.0
epsilon = 1e-06
LOG2E = math.log2(math.e)
BLOCKED = -1e30

P2, P1, N1, N2 = 0, 1, 2, 3
OFFSET = (-2, -1, 1, 2)
SIB = 8
PIECES = 4
TILE = 256


def kernel(row_total, col_total, e_ref, counts_ref, pairs_ref, dens_ref, out_ref,
           held, acc, tot, scale, send_own, send_link, send_sib, recv):
    rows, width = e_ref.shape
    piece = rows // PIECES
    tiles = rows // TILE
    pieces_per_tile = PIECES // tiles
    chips = col_total // 2
    chip_total = row_total * chips
    block_total = row_total * col_total
    row = lax.axis_index("row")
    col = lax.axis_index("col")
    z = col // 2
    core = col % 2
    chip = row * chips + z
    me = row * col_total + col
    lines = chips == 4 and row_total >= 3

    def device(where, lane):
        where = lax.rem(where + 2 * chip_total, chip_total)
        return {"row": where // chips, "col": lax.rem(where, chips) * 2 + lane}

    sibling = device(chip, 1 - core)
    above = device(chip + 1, core)
    below = device(chip - 1, core)
    next_line = device(chip + chips, core)
    last_line = device(chip - chips, core)

    def when(condition, action):
        if condition is True:
            action()
        elif condition is not False:
            pl.when(condition)(action)

    if lines:
        has_below, has_above = z > 0, z < 3
        middle = (z == 1) | (z == 2)
        low, high = z < 2, z >= 2
        ends = (z == 0) | (z == 3)
    else:
        has_below = has_above = middle = True

    barrier = pltpu.get_barrier_semaphore()

    def greet(who):
        pl.semaphore_signal(barrier, inc=1, device_id=who, device_id_type=MESH)

    greet(sibling)
    when(has_above, lambda: greet(above))
    when(has_below, lambda: greet(below))
    if lines:
        greet(next_line)
        greet(last_line)
        when(middle, lambda: pl.semaphore_wait(barrier, 5))
        when(ends, lambda: pl.semaphore_wait(barrier, 4))
    else:
        pl.semaphore_wait(barrier, 3)

    def part(k):
        return pl.ds(pl.multiple_of(k * piece, piece), piece)

    def copy(src, slot, k, send, who):
        return pltpu.make_async_remote_copy(
            src_ref=src.at[part(k)], dst_ref=held.at[slot, part(k)],
            send_sem=send.at[k], recv_sem=recv.at[slot, k],
            device_id=who, device_id_type=MESH)

    mine = core * 4
    other = (1 - core) * 4

    def own_up(k):
        return copy(e_ref, mine + P1, k, send_own.at[0], above)

    def own_down(k):
        return copy(e_ref, mine + N1, k, send_own.at[1], below)

    def own_sib(k):
        return copy(e_ref, SIB, k, send_own.at[2], sibling)

    def relay(slot, to_slot, k, who):
        return copy(held.at[mine + slot], mine + to_slot, k, send_link.at[slot], who)

    def share(slot, k):
        return copy(held.at[mine + slot], mine + slot, k, send_sib.at[slot], sibling)

    def await_piece(slot, k):
        copy(e_ref, slot, k, send_own.at[0], sibling).wait_recv()

    def each(n, action):
        lax.fori_loop(0, n, lambda k, c: (action(k), c)[1], 0)

    def start_own(k):
        when(has_below, lambda: own_down(k).start())
        when(has_above, lambda: own_up(k).start())
        own_sib(k).start()

    each(PIECES, start_own)

    def limit(block):
        listed = jnp.int32(0)
        for j in range(pairs_ref.shape[1]):
            listed = listed | jnp.where(pairs_ref[me, j] == block, 1, 0)
        return counts_ref[block] * listed

    def inverse(x):
        x = x.astype(jnp.float32)
        return lax.rsqrt(jnp.sum(x * x, axis=1, keepdims=True) + epsilon)

    def one_tile(x, block, t):
        size = x.shape[0]
        column = jnp.transpose(jnp.broadcast_to(inverse(x), (size, 128)))[0:1, :]
        slot_index = lax.broadcasted_iota(jnp.int32, (1, size), 1) + t * TILE
        shift = jnp.where(slot_index < limit(block), -smoothing_scale * LOG2E, BLOCKED)
        products = lax.dot_general(
            e_ref[...], x, (((1,), (1,)), ((), ())), preferred_element_type=jnp.float32)
        weight = jnp.exp2(products * scale[...] * column + shift)
        folded = weight[:, :128]
        for j in range(1, size // 128):
            folded = folded + weight[:, j * 128:(j + 1) * 128]
        tot[...] += folded
        acc[...] += jnp.dot(weight.astype(jnp.bfloat16), x, preferred_element_type=jnp.float32)

    def tile_rows(t):
        return pl.ds(pl.multiple_of(t * TILE, TILE), TILE)

    def held_tile(slot, block, t):
        one_tile(held[slot, tile_rows(t), :], block, t)

    def owner(slot, lane):
        return lax.rem(chip * 2 + 2 * offset_of(slot) + lane + block_total, block_total)

    def offset_of(slot):
        if isinstance(slot, int):
            return OFFSET[slot]
        return slot - 2 + slot // 2

    def own_lane_tile(slot, t):
        held_tile(mine + slot, owner(slot, core), t)

    def other_lane_tile(slot, t):
        for j in range(pieces_per_tile):
            await_piece(other + slot, t * pieces_per_tile + j)
        held_tile(other + slot, owner(slot, 1 - core), t)

    def both_tiles(slot, t):
        def go(lane, c):
            here = lax.rem(core + lane, 2)

            @pl.when(lane == 1)
            def _():
                for j in range(pieces_per_tile):
                    await_piece(here * 4 + slot, t * pieces_per_tile + j)

            held_tile(here * 4 + slot, owner(slot, here), t)
            return c

        lax.fori_loop(0, 2, go, 0)

    scale[...] = jnp.broadcast_to(
        inverse(e_ref[...]) * (smoothing_scale * LOG2E), scale.shape)
    acc[...] = jnp.zeros_like(acc)
    tot[...] = jnp.zeros_like(tot)

    each(tiles, lambda t: one_tile(e_ref[tile_rows(t), :], me, t))

    def sib_tile(t):
        for j in range(pieces_per_tile):
            await_piece(SIB, t * pieces_per_tile + j)
        held_tile(SIB, me + 1 - 2 * core, t)

    each(tiles, sib_tile)

    def near(k):
        def from_above():
            await_piece(mine + N1, k)
            when(middle, lambda: relay(N1, N2, k, below).start())
            share(N1, k).start()

        def from_below():
            await_piece(mine + P1, k)
            when(middle, lambda: relay(P1, P2, k, above).start())
            share(P1, k).start()

        when(has_above, from_above)
        when(has_below, from_below)

    each(PIECES, near)

    per = PIECES // tiles

    def take_far_above(k):
        await_piece(mine + N2, k)
        if lines:
            when(low, lambda: relay(N2, P2, k, next_line).start())
            when(z == 2, lambda: relay(N2, N1, k, above).start())
        when(core == 0, lambda: share(N2, k).start())

    def take_far_below(k):
        await_piece(mine + P2, k)
        if lines:
            when(high, lambda: relay(P2, N2, k, last_line).start())
            when(z == 1, lambda: relay(P2, P1, k, below).start())
        when(core == 1, lambda: share(P2, k).start())

    def far(k):
        if lines:
            when(high, lambda: take_far_below(k))
            take_far_above(k)
            when(low, lambda: take_far_below(k))
        else:
            take_far_above(k)
            take_far_below(k)

    def spread(k, slots, job):
        steps = PIECES // 2
        t_per = tiles // steps if tiles >= steps else 1
        which = k // steps
        base = (k % steps) * t_per
        for j in range(t_per):
            job(slots(which), base + j)

    def second(k):
        far(k)
        slot = N1 - k // (PIECES // 2)
        t = k % (PIECES // 2)
        if lines:
            skip = ((z == 0) & (slot == P1)) | ((z == 3) & (slot == N1))
            when(jnp.logical_not(skip), lambda: both_tiles(slot, t))
        else:
            both_tiles(slot, t)

    each(PIECES, second)

    if lines:
        last = jnp.where(z == 0, P1, N1)

    def third(k):
        if lines:
            def take():
                await_piece(mine + last, k)
                share_last(k).start()

            when(ends, take)
        slot = N2 * (k // (PIECES // 2))
        t = k % (PIECES // 2)
        own_lane_tile(slot, t)

    def share_last(k):
        return copy(held.at[mine + last], mine + last, k, send_sib.at[last], sibling)

    def far_other(t):
        slot = N2 * core
        other_lane_tile(slot, t)

    each(tiles, far_other) if not lines else None
    if lines:
        def third_all(k):
            third(k)
            when((k % 2) == 0, lambda: far_other(k // 2))
            when(ends & (k == PIECES - 1), lambda: both_tiles(last, 0))

        each(PIECES, third_all)
        when(ends, lambda: both_tiles(last, tiles - 1))
    else:
        each(PIECES, third)

    total = jnp.sum(tot[...], axis=1, keepdims=True)
    count = counts_ref[me]
    valid = lax.broadcasted_iota(jnp.int32, (rows, 1), 0) < count
    out_ref[...] = jnp.where(valid, acc[...] / total, 0.0).astype(out_ref.dtype)
    across = jnp.transpose(jnp.broadcast_to(total, (rows, 128)))[0:1, :]
    dens_ref[...] = jnp.where(
        lax.broadcasted_iota(jnp.int32, (1, rows), 1) < count, across, 0.0)

    def drain(k):
        when(has_below, lambda: own_down(k).wait_send())
        when(has_above, lambda: own_up(k).wait_send())
        own_sib(k).wait_send()
        when(middle, lambda: relay(N1, N2, k, below).wait_send())
        when(middle, lambda: relay(P1, P2, k, above).wait_send())
        share(N1, k).wait_send()
        share(P1, k).wait_send()
        when(core == 0, lambda: share(N2, k).wait_send())
        when(core == 1, lambda: share(P2, k).wait_send())
        if lines:
            when(z < 3, lambda: relay(N2, P2, k, next_line).wait_send())
            when(z > 0, lambda: relay(P2, N2, k, last_line).wait_send())

    each(PIECES, drain)


def solution(mesh):
    row_total, col_total = mesh.shape["row"], mesh.shape["col"]

    def body(embeddings, counts, pairs):
        rows, width = embeddings.shape
        density, neighbour = pl.pallas_call(
            functools.partial(kernel, row_total, col_total),
            out_shape=(jax.ShapeDtypeStruct((1, rows), jnp.float32),
                       jax.ShapeDtypeStruct((rows, width), jnp.bfloat16)),
            in_specs=[pl.BlockSpec(memory_space=pltpu.VMEM),
                      pl.BlockSpec(memory_space=pltpu.SMEM),
                      pl.BlockSpec(memory_space=pltpu.SMEM)],
            out_specs=(pl.BlockSpec(memory_space=pltpu.VMEM),
                       pl.BlockSpec(memory_space=pltpu.VMEM)),
            scratch_shapes=[
                pltpu.VMEM((9, rows, width), jnp.bfloat16),
                pltpu.VMEM((rows, width), jnp.float32),
                pltpu.VMEM((rows, 128), jnp.float32),
                pltpu.VMEM((rows, TILE), jnp.float32),
                pltpu.SemaphoreType.DMA((3, PIECES)),
                pltpu.SemaphoreType.DMA((4, PIECES)),
                pltpu.SemaphoreType.DMA((4, PIECES)),
                pltpu.SemaphoreType.DMA((9, PIECES)),
            ],
            compiler_params=pltpu.CompilerParams(
                collective_id=0, has_side_effects=True, vmem_limit_bytes=48 * 1024 * 1024),
        )(embeddings, counts, pairs)
        return density.reshape(rows), neighbour

    in_specs = (P(("row", "col"), None), P(), P())
    out_specs = (P(("row", "col")), P(("row", "col"), None))
    return jax.shard_map(body, mesh=mesh, in_specs=in_specs, out_specs=out_specs, check_vma=False)
```

```python
import functools
import math

import jax
import jax.numpy as jnp
from jax import lax
from jax.experimental import pallas as pl
from jax.experimental.pallas import tpu as pltpu
from jax.sharding import PartitionSpec as P

MESH = pl.DeviceIdType.MESH

smoothing_scale = 4.0
epsilon = 1e-06
LOG2E = math.log2(math.e)
BLOCKED = -1e30

P2, P1, N1, N2 = 0, 1, 2, 3
OFFSET = (-2, -1, 1, 2)
SIB = 8
PIECES = 4


def kernel(row_total, col_total, e_hbm, counts_ref, pairs_hbm, dens_ref, out_ref,
           e_ref, pairs_ref, held, acc, tot, scale, local, send_own, send_link, send_sib, recv):
    rows, width = e_ref.shape
    piece = rows // PIECES
    chips = col_total // 2
    chip_total = row_total * chips
    block_total = row_total * col_total
    row = lax.axis_index("row")
    col = lax.axis_index("col")
    z = col // 2
    core = col % 2
    chip = row * chips + z
    me = row * col_total + col
    lines = chips == 4 and row_total >= 3

    def device(where, lane):
        where = lax.rem(where + 2 * chip_total, chip_total)
        return {"row": where // chips, "col": lax.rem(where, chips) * 2 + lane}

    sibling = device(chip, 1 - core)
    above = device(chip + 1, core)
    below = device(chip - 1, core)
    next_line = device(chip + chips, core)
    last_line = device(chip - chips, core)

    def when(condition, action):
        if condition is True:
            action()
        elif condition is not False:
            pl.when(condition)(action)

    if lines:
        has_below, has_above = z > 0, z < 3
        middle = (z == 1) | (z == 2)
        low, high = z < 2, z >= 2
        ends = (z == 0) | (z == 3)
    else:
        has_below = has_above = middle = True

    load_own = pltpu.make_async_copy(e_hbm, e_ref, local.at[0])
    load_pairs = pltpu.make_async_copy(pairs_hbm, pairs_ref, local.at[1])
    load_own.start()
    load_pairs.start()
    barrier = pltpu.get_barrier_semaphore()

    def greet(who):
        pl.semaphore_signal(barrier, inc=1, device_id=who, device_id_type=MESH)

    greet(sibling)
    when(has_above, lambda: greet(above))
    when(has_below, lambda: greet(below))
    if lines:
        greet(next_line)
        greet(last_line)
        when(middle, lambda: pl.semaphore_wait(barrier, 5))
        when(ends, lambda: pl.semaphore_wait(barrier, 4))
    else:
        pl.semaphore_wait(barrier, 3)

    def part(k):
        return pl.ds(pl.multiple_of(k * piece, piece), piece)

    def copy(src, slot, k, send, who):
        return pltpu.make_async_remote_copy(
            src_ref=src.at[part(k)], dst_ref=held.at[slot, part(k)],
            send_sem=send.at[k], recv_sem=recv.at[slot, k],
            device_id=who, device_id_type=MESH)

    mine = core * 4
    other = (1 - core) * 4

    def own_up(k):
        return copy(e_hbm, mine + P1, k, send_own.at[0], above)

    def own_down(k):
        return copy(e_hbm, mine + N1, k, send_own.at[1], below)

    def own_sib(k):
        return copy(e_hbm, SIB, k, send_own.at[2], sibling)

    def relay(slot, to_slot, k, who):
        return copy(held.at[mine + slot], mine + to_slot, k, send_link.at[slot], who)

    def share(slot, k):
        return copy(held.at[mine + slot], mine + slot, k, send_sib.at[slot], sibling)

    def await_piece(slot, k):
        copy(e_hbm, slot, k, send_own.at[0], sibling).wait_recv()

    def each(n, action):
        lax.fori_loop(0, n, lambda k, c: (action(k), c)[1], 0)

    def start_own(k):
        when(has_below, lambda: own_down(k).start())
        when(has_above, lambda: own_up(k).start())
        own_sib(k).start()

    each(PIECES, start_own)
    load_own.wait()
    load_pairs.wait()

    def limit(block):
        listed = jnp.int32(0)
        for j in range(pairs_ref.shape[1]):
            listed = listed | jnp.where(pairs_ref[me, j] == block, 1, 0)
        return counts_ref[block] * listed

    def inverse(x):
        x = x.astype(jnp.float32)
        return lax.rsqrt(jnp.sum(x * x, axis=1, keepdims=True) + epsilon)

    def one_tile(x, bounds, first):
        size = x.shape[0]
        column = jnp.transpose(jnp.broadcast_to(inverse(x), (size, 128)))[0:1, :]
        span = size // len(bounds)
        slot_index = lax.broadcasted_iota(jnp.int32, (1, span), 1) + first
        valid = [slot_index < bound for bound in bounds]
        shift = jnp.concatenate(
            [jnp.where(v, -smoothing_scale * LOG2E, BLOCKED) for v in valid], axis=1)
        products = lax.dot_general(
            e_ref[...], x, (((1,), (1,)), ((), ())), preferred_element_type=jnp.float32)
        weight = jnp.exp2(products * scale[...] * column + shift)
        folded = weight[:, :128]
        for j in range(1, size // 128):
            folded = folded + weight[:, j * 128:(j + 1) * 128]
        tot[...] += folded
        acc[...] += jnp.dot(weight.astype(jnp.bfloat16), x, preferred_element_type=jnp.float32)

    def block_tile(slot, block):
        one_tile(held[slot], [limit(block)], 0)

    def owner(slot, lane):
        return lax.rem(chip * 2 + 2 * offset_of(slot) + lane + block_total, block_total)

    def offset_of(slot):
        if isinstance(slot, int):
            return OFFSET[slot]
        return slot - 2 + slot // 2

    def await_block(slot):
        each(PIECES, lambda k: await_piece(slot, k))

    def lane_tile(slot, shared):
        lane = lax.rem(core + shared, 2)
        pl.when(shared == 1)(lambda: await_block(lane * 4 + slot))
        block_tile(lane * 4 + slot, owner(slot, lane))

    scale[...] = jnp.broadcast_to(
        inverse(e_ref[...]) * (smoothing_scale * LOG2E), scale.shape)
    acc[...] = jnp.zeros_like(acc)
    tot[...] = jnp.zeros_like(tot)

    one_tile(e_ref[...], [limit(me)], 0)
    await_block(SIB)
    block_tile(SIB, me + 1 - 2 * core)

    def near(k):
        def from_above():
            await_piece(mine + N1, k)
            when(middle, lambda: relay(N1, N2, k, below).start())
            share(N1, k).start()

        def from_below():
            await_piece(mine + P1, k)
            when(middle, lambda: relay(P1, P2, k, above).start())
            share(P1, k).start()

        when(has_above, from_above)
        when(has_below, from_below)

    each(PIECES, near)


    def take_far_above(k):
        await_piece(mine + N2, k)
        if lines:
            when(low, lambda: relay(N2, P2, k, next_line).start())
            when(z == 2, lambda: relay(N2, N1, k, above).start())
        when(core == 0, lambda: share(N2, k).start())

    def take_far_below(k):
        await_piece(mine + P2, k)
        if lines:
            when(high, lambda: relay(P2, N2, k, last_line).start())
            when(z == 1, lambda: relay(P2, P1, k, below).start())
        when(core == 1, lambda: share(P2, k).start())

    def far(k):
        if lines:
            when(high, lambda: take_far_below(k))
            take_far_above(k)
            when(low, lambda: take_far_below(k))
        else:
            take_far_above(k)
            take_far_below(k)

    group = 4 // PIECES

    def near_tile(job):
        slot = N1 - job // 2
        if lines:
            skip = ((z == 0) & (slot == P1)) | ((z == 3) & (slot == N1))
            when(jnp.logical_not(skip), lambda: lane_tile(slot, job % 2))
        else:
            lane_tile(slot, job % 2)

    def second(k):
        far(k)
        for j in range(group):
            near_tile(k * group + j)

    each(PIECES, second)

    def far_tile(job):
        slot = jnp.where(job == 2, N2 * core, N2 * job)
        lane_tile(slot, job // 2)

    if lines:
        last = jnp.where(z == 0, P1, N1)
        half = rows // 2

        def share_last(k):
            return copy(held.at[mine + last], mine + last, k, send_sib.at[last], sibling)

        def last_tile(h):
            for j in range(PIECES // 2):
                await_piece(other + last, h * (PIECES // 2) + j)
            here = pl.ds(pl.multiple_of(h * half, half), half)
            x = jnp.concatenate([held[mine + last, here, :], held[other + last, here, :]], axis=0)
            one_tile(x, [limit(owner(last, core)), limit(owner(last, 1 - core))], h * half)

        def third(q):
            when(q < 3, lambda: far_tile(q))
            when(ends & (q == 3), lambda: last_tile(q - 3))

            def take():
                await_piece(mine + last, q // group)
                share_last(q // group).start()

            when(ends if group == 1 else ends & (q % 2 == 1), take)

        each(4, third)
        when(ends, lambda: last_tile(core * 0 + 1))
    else:
        each(3, far_tile)

    total = jnp.sum(tot[...], axis=1, keepdims=True)
    count = counts_ref[me]
    valid = lax.broadcasted_iota(jnp.int32, (rows, 1), 0) < count
    out_ref[...] = jnp.where(valid, acc[...] * (1.0 / total), 0.0).astype(out_ref.dtype)
    across = jnp.transpose(jnp.broadcast_to(total, (rows, 128)))[0:1, :]
    dens_ref[...] = jnp.where(
        lax.broadcasted_iota(jnp.int32, (1, rows), 1) < count, across, 0.0)

    def drain(k):
        when(has_below, lambda: own_down(k).wait_send())
        when(has_above, lambda: own_up(k).wait_send())
        own_sib(k).wait_send()
        when(middle, lambda: relay(N1, N2, k, below).wait_send())
        when(middle, lambda: relay(P1, P2, k, above).wait_send())
        share(N1, k).wait_send()
        share(P1, k).wait_send()
        when(core == 0, lambda: share(N2, k).wait_send())
        when(core == 1, lambda: share(P2, k).wait_send())
        if lines:
            when(z < 3, lambda: relay(N2, P2, k, next_line).wait_send())
            when(z > 0, lambda: relay(P2, N2, k, last_line).wait_send())

    each(PIECES, drain)


def solution(mesh):
    row_total, col_total = mesh.shape["row"], mesh.shape["col"]

    def body(embeddings, counts, pairs):
        rows, width = embeddings.shape
        density, neighbour = pl.pallas_call(
            functools.partial(kernel, row_total, col_total),
            out_shape=(jax.ShapeDtypeStruct((1, rows), jnp.float32),
                       jax.ShapeDtypeStruct((rows, width), jnp.bfloat16)),
            in_specs=[pl.BlockSpec(memory_space=pltpu.HBM),
                      pl.BlockSpec(memory_space=pltpu.SMEM),
                      pl.BlockSpec(memory_space=pltpu.HBM)],
            out_specs=(pl.BlockSpec(memory_space=pltpu.VMEM),
                       pl.BlockSpec(memory_space=pltpu.VMEM)),
            scratch_shapes=[
                pltpu.VMEM((rows, width), jnp.bfloat16),
                pltpu.SMEM(pairs.shape, jnp.int32),
                pltpu.VMEM((9, rows, width), jnp.bfloat16),
                pltpu.VMEM((rows, width), jnp.float32),
                pltpu.VMEM((rows, 128), jnp.float32),
                pltpu.VMEM((rows, rows), jnp.float32),
                pltpu.SemaphoreType.DMA((2,)),
                pltpu.SemaphoreType.DMA((3, PIECES)),
                pltpu.SemaphoreType.DMA((4, PIECES)),
                pltpu.SemaphoreType.DMA((4, PIECES)),
                pltpu.SemaphoreType.DMA((9, PIECES)),
            ],
            compiler_params=pltpu.CompilerParams(
                collective_id=0, has_side_effects=True, vmem_limit_bytes=48 * 1024 * 1024),
        )(embeddings, counts, pairs)
        return density.reshape(rows), neighbour

    in_specs = (P(("row", "col"), None), P(), P())
    out_specs = (P(("row", "col")), P(("row", "col"), None))
    return jax.shard_map(body, mesh=mesh, in_specs=in_specs, out_specs=out_specs, check_vma=False)
```
